32 devices in a mesh: dp: 2 (over core), tm: 4 (over y, x), space: 4 (over z).
Axes of the slice: x: 2, y: 2, z: 4, core: 2. Of those that a mesh axis runs over, the one named last changes fastest.
Arguments:
- clip_latent: bfloat16 [2, 8, 64, 32, 256], P('dp', 'tm', 'space'), may hold values from -6 to 6
- grad_out: bfloat16 [2, 4, 64, 32, 256], P('dp', 'tm', 'space'), may hold values from -6 to 6
- w_spatial: bfloat16 [2304, 256], replicated, may hold values from -0.125 to 0.125
- w_temporal: bfloat16 [768, 256], replicated, may hold values from -0.21875 to 0.21875
- w_down: bfloat16 [768, 256], replicated, may hold values from -0.21875 to 0.21875
Outputs:
- latent_grad: bfloat16 [2, 8, 64, 32, 256], P('dp', 'tm', 'space')
- grad_spatial: float32 [256, 2304], P('space', ('dp', 'tm'))
- grad_temporal: float32 [256, 768], P('space', ('dp', 'tm'))
- grad_down: float32 [256, 768], P('space', ('dp', 'tm'))
The draws below stay inside these ranges and needn't reach their ends.
All inputs are finite; a program needn't handle non-finite values.
Results may differ from the reference program's by a relative error of at most 0.0052.
Values may be sent and summed in bfloat16 or wider, within the bound.
A program may use at most 64 MiB of HBM per device.

```python
import math
import jax
import jax.numpy as jnp

C = 256
COLS = 32
CLIPS = 2
FRAMES = 8
ROWS = 64


def spiked(values, stream_key, source, target, blocks, factor):
    owner, partner = [(jnp.arange(values.shape[position]) // (values.shape[position] // blocks)).reshape([-1 if axis == position else 1 for axis in range(values.ndim)]) for position in (source, target)]
    chosen = jax.random.permutation(stream_key, blocks)[partner]
    strong = (owner == chosen) | (owner == (partner + blocks // 2) % blocks)
    return jnp.where(strong, factor * values, values)


def block_levels(rng, extent, split, low, largest):
    level, own = 1.0, jax.random.fold_in(rng, 6)
    for dim, blocks in split:
        heights = jnp.exp(jax.random.uniform(jax.random.fold_in(own, dim), (blocks,), jnp.float32, low / len(split), largest / len(split)))
        level = level * jnp.repeat(heights, extent[dim] // blocks).reshape([-1 if axis == dim else 1 for axis in range(len(extent))])
    return level


def scatter_about(key, extent, width, most, cuts=(), kind=jnp.bfloat16):
    values = jax.random.normal(key, extent, jnp.float32) * width
    if len(cuts) > 0:
        values = block_levels(key, extent, cuts, -0.22, 0.18) * values
    return jnp.clip(values, min=-most, max=most).astype(kind)


def heavy_noise(stream_key, shape, width, most, shards, heavy, dtype=jnp.bfloat16):
    array = width * jax.random.normal(stream_key, shape, jnp.float32)
    if shards:
        array = array * block_levels(stream_key, shape, shards, -0.22, 0.18)
    return jnp.clip(spiked(array, jax.random.fold_in(stream_key, 3), *heavy), -most, most).astype(dtype)


def setup_inputs(seed: int = 0) -> dict:
    key_of = jax.random.split(jax.random.key(seed), 6)
    clip_latent = scatter_about(key_of[0], (CLIPS, FRAMES, ROWS, COLS, C), 1.0, 6.0, ((0, 2), (1, 4), (2, 4)))
    grad_out = heavy_noise(key_of[1], (CLIPS, FRAMES // 2, ROWS, COLS, C), 1.0, 6.0, ((0, 2), (1, 4), (2, 4)), (2, 4, 4, 2.0))
    w_spatial = scatter_about(key_of[2], (9 * C, C), (9 * C) ** -0.5, 0.125)
    w_temporal = scatter_about(key_of[3], (3 * C, C), (3 * C) ** -0.5, 0.21875)
    w_down = scatter_about(key_of[4], (3 * C, C), (3 * C) ** -0.5, 0.21875)
    return {"clip_latent": clip_latent, "grad_out": grad_out, "w_spatial": w_spatial, "w_temporal": w_temporal, "w_down": w_down}


def past_frames(values, lag):
    if lag == 0:
        return values
    zeros = jnp.zeros_like(values[:, :lag])
    return jnp.concatenate([zeros, values[:, :-lag]], axis=1)

def next_frames(values, lead):
    if lead == 0:
        return values
    zeros = jnp.zeros_like(values[:, :lead])
    return jnp.concatenate([values[:, lead:], zeros], axis=1)

def product(values, matrix):
    flat = values.reshape(-1, values.shape[-1])
    result = jnp.dot(flat, matrix, preferred_element_type=jnp.float32)
    return result.reshape(values.shape[:-1] + (matrix.shape[1],))

def gram(left, right):
    flat_left = left.reshape(-1, left.shape[-1])
    flat_right = right.reshape(-1, right.shape[-1])
    return jnp.dot(flat_left.T, flat_right, preferred_element_type=jnp.float32)

def reference(clip_latent, grad_out, w_spatial, w_temporal, w_down):
    chans = clip_latent.shape[-1]
    rows = clip_latent.shape[2]
    cols = clip_latent.shape[3]

    def block(weight, index):
        return weight[index * chans:(index + 1) * chans]
    widths = ((0, 0), (0, 0), (1, 1), (1, 1), (0, 0))
    padded_x = jnp.pad(clip_latent, widths)
    pre_act = jnp.zeros(clip_latent.shape, jnp.float32)
    for index in range(9):
        i, j = (index // 3, index % 3)
        pre_act = pre_act + product(padded_x[:, :, i:i + rows, j:j + cols], block(w_spatial, index))
    hidden = jax.nn.silu(pre_act).astype(jnp.bfloat16)
    temporal_sum = jnp.zeros(clip_latent.shape, jnp.float32)
    for k in range(3):
        temporal_sum = temporal_sum + product(past_frames(hidden, 2 - k), block(w_temporal, k))
    mixed = (clip_latent.astype(jnp.float32) + temporal_sum).astype(jnp.bfloat16)
    spread = jnp.stack([grad_out, jnp.zeros_like(grad_out)], axis=2).reshape(clip_latent.shape)
    mixed_wide = jnp.zeros(clip_latent.shape, jnp.float32)
    for k in range(3):
        mixed_wide = mixed_wide + product(next_frames(spread, 2 - k), block(w_down, k).T)
    mixed_grad = mixed_wide.astype(jnp.bfloat16)
    hidden_grad = jnp.zeros(clip_latent.shape, jnp.float32)
    for k in range(3):
        hidden_grad = hidden_grad + product(next_frames(mixed_grad, 2 - k), block(w_temporal, k).T)
    sigma = jax.nn.sigmoid(pre_act)
    act_grad = (hidden_grad * sigma * (1.0 + pre_act * (1.0 - sigma))).astype(jnp.bfloat16)
    padded_da = jnp.pad(act_grad, widths)
    latent_wide = mixed_grad.astype(jnp.float32)
    for index in range(9):
        i, j = (index // 3, index % 3)
        latent_wide = latent_wide + product(padded_da[:, :, 2 - i:2 - i + rows, 2 - j:2 - j + cols], block(w_spatial, index).T)
    latent_grad = latent_wide.astype(jnp.bfloat16)
    scale = 1.0 / math.sqrt(CLIPS * FRAMES * ROWS * COLS)
    spatial_parts = []
    for index in range(9):
        i, j = (index // 3, index % 3)
        spatial_parts.append(gram(act_grad, padded_x[:, :, i:i + rows, j:j + cols]))
    grad_spatial = scale * jnp.concatenate(spatial_parts, axis=1)
    grad_temporal = scale * jnp.concatenate([gram(mixed_grad, past_frames(hidden, 2 - k)) for k in range(3)], axis=1)
    grad_down = scale * jnp.concatenate([gram(grad_out, past_frames(mixed, 2 - k)[:, ::2]) for k in range(3)], axis=1)
    return (latent_grad, grad_spatial, grad_temporal, grad_down)
```

```python
import functools
import math

import jax
import jax.numpy as jnp
from jax import lax
from jax.experimental import pallas as pl
from jax.experimental.pallas import tpu as pltpu
from jax.sharding import PartitionSpec as P


def padded_2(cells, sides, width):
    for axis, dim in sides:
        count = lax.axis_size(axis)
        ends = count - 1
        head = lax.slice_in_dim(cells, 0, width, axis=dim)
        tail = lax.slice_in_dim(cells, cells.shape[dim] - width, cells.shape[dim], axis=dim)
        cells = jnp.concatenate(
            [
                lax.ppermute(tail, axis, [(i, (i + 1) % count) for i in range(ends)]),
                cells,
                lax.ppermute(head, axis, [((i + 1) % count, i) for i in range(ends)]),
            ],
            axis=dim,
        )
    return cells


def from_behind(block, axis, distance):
    devices = range(lax.axis_size(axis))
    route = [(i - distance, i) for i in devices if i - distance in devices]
    return lax.ppermute(block, axis, route)


def merge_cells(values):
    return values.reshape(-1, values.shape[-1])


def pad_columns(values):
    return jnp.pad(values, ((0, 0), (0, 0), (0, 0), (1, 1), (0, 0)))


def spatial_columns(padded, rows, cols, flipped):
    pieces = []
    for i in range(3):
        for j in range(3):
            top = 2 - i if flipped else i
            left = 2 - j if flipped else j
            pieces.append(padded[:, :, top : top + rows, left : left + cols])
    return merge_cells(jnp.concatenate(pieces, axis=-1))


def frame_columns(extended, count, offsets):
    return merge_cells(jnp.concatenate([extended[:, o : o + count] for o in offsets], axis=-1))


def flip_blocks(weight, taps):
    chans = weight.shape[1]
    return weight.reshape(taps, chans, chans).transpose(0, 2, 1).reshape(taps * chans, chans)


def causal_mix(past, current, weight):
    extended = jnp.concatenate([past, current], axis=1)
    columns = frame_columns(extended, current.shape[1], (0, 1, 2))
    summed = jnp.dot(columns, weight, preferred_element_type=jnp.float32)
    return summed.reshape(current.shape)


def round_up(size, step):
    return (size + step - 1) // step * step


def reduce_kernel(
    groups,
    bands,
    scale,
    parts_ref,
    out_ref,
    from_core,
    mid,
    from_group,
    total,
    turned,
    turned_wide,
    from_band,
    core_send,
    core_recv,
    group_send,
    group_recv,
    band_send,
    band_recv,
):
    core = lax.axis_index("dp")
    group = lax.axis_index("tm")
    band = lax.axis_index("space")
    rows = parts_ref.shape[2]
    chans = parts_ref.shape[3]

    def at(d, t, s):
        return dict(device_id=(d, t, s), device_id_type=pl.DeviceIdType.MESH)

    barrier = pltpu.get_barrier_semaphore()
    pl.semaphore_signal(barrier, inc=1, **at(1 - core, group, band))
    for i in range(groups - 1):
        pl.semaphore_signal(barrier, inc=1, **at(core, lax.rem(group + 1 + i, groups), band))
    for i in range(bands - 1):
        pl.semaphore_signal(barrier, inc=1, **at(core, group, lax.rem(band + 1 + i, bands)))
    pl.semaphore_wait(barrier, groups + bands - 1)

    core_copies = []
    for i in range(groups):
        target = lax.rem(group + 1 + i, groups)
        copy = pltpu.make_async_remote_copy(
            src_ref=parts_ref.at[1 - core, target],
            dst_ref=from_core.at[i],
            send_sem=core_send.at[i],
            recv_sem=core_recv.at[i],
            **at(1 - core, group, band),
        )
        copy.start()
        core_copies.append(copy)

    group_copies = []
    for i in range(groups):
        target = lax.rem(group + 1 + i, groups)
        core_copies[i].wait_recv()
        summed = parts_ref[core, target].astype(jnp.float32) + from_core[i].astype(jnp.float32)
        if i == groups - 1:
            total[0:rows, :] = summed
        else:
            mid[i] = summed.astype(jnp.bfloat16)
            copy = pltpu.make_async_remote_copy(
                src_ref=mid.at[i],
                dst_ref=from_group.at[i],
                send_sem=group_send.at[i],
                recv_sem=group_recv.at[i],
                **at(core, target, band),
            )
            copy.start()
            group_copies.append(copy)
    if total.shape[0] > rows:
        total[rows:, :] = jnp.zeros((total.shape[0] - rows, chans), jnp.float32)
    for i in range(groups - 1):
        group_copies[i].wait_recv()
        total[0:rows, :] += from_group[i].astype(jnp.float32)

    flat = (total[...] * scale).T.reshape(turned.shape)
    turned_wide[...] = flat
    turned[...] = flat.astype(jnp.bfloat16)
    band_copies = []
    for i in range(bands - 1):
        target = lax.rem(band + 1 + i, bands)
        copy = pltpu.make_async_remote_copy(
            src_ref=turned.at[target],
            dst_ref=from_band.at[i],
            send_sem=band_send.at[i],
            recv_sem=band_recv.at[i],
            **at(core, group, target),
        )
        copy.start()
        band_copies.append(copy)
    result = turned_wide[band]
    for i in range(bands - 1):
        band_copies[i].wait_recv()
        result += from_band[i].astype(jnp.float32)
    out_ref[...] = result
    for copy in core_copies + group_copies + band_copies:
        copy.wait_send()


def reduce_parts(parts, scale):
    cores, groups, rows, chans = parts.shape
    bands = lax.axis_size("space")
    wide = round_up(rows, 128)
    share = chans // bands
    dma = pltpu.SemaphoreType.DMA
    return pl.pallas_call(
        functools.partial(reduce_kernel, groups, bands, scale),
        out_shape=jax.ShapeDtypeStruct((share, wide), jnp.float32),
        in_specs=[pl.BlockSpec(memory_space=pltpu.VMEM)],
        out_specs=pl.BlockSpec(memory_space=pltpu.VMEM),
        scratch_shapes=[
            pltpu.VMEM((groups, rows, chans), jnp.bfloat16),
            pltpu.VMEM((groups - 1, rows, chans), jnp.bfloat16),
            pltpu.VMEM((groups - 1, rows, chans), jnp.bfloat16),
            pltpu.VMEM((wide, chans), jnp.float32),
            pltpu.VMEM((bands, share, wide), jnp.bfloat16),
            pltpu.VMEM((bands, share, wide), jnp.float32),
            pltpu.VMEM((bands - 1, share, wide), jnp.bfloat16),
            dma((groups,)),
            dma((groups,)),
            dma((groups - 1,)),
            dma((groups - 1,)),
            dma((bands - 1,)),
            dma((bands - 1,)),
        ],
        compiler_params=pltpu.CompilerParams(
            collective_id=0, has_side_effects=True, vmem_limit_bytes=40 * 1024 * 1024
        ),
    )(parts)


def per_device(clip_latent, grad_out, w_spatial, w_temporal, w_down):
    clips, frames, rows, cols, chans = clip_latent.shape
    assert frames == 2 and grad_out.shape[1] == 1
    groups = lax.axis_size("tm")
    cores = lax.axis_size("dp")
    total = clips * frames * rows * cols * cores * groups * lax.axis_size("space")
    scale = 1.0 / math.sqrt(total)
    rim_latent = padded_2(clip_latent, (("space", 2),), 1)
    next_grad = from_behind(grad_out, "tm", -1)
    later_grad = from_behind(grad_out, "tm", -2)
    columns_x = spatial_columns(pad_columns(rim_latent), rows, cols, False)
    pre_act = jnp.dot(columns_x, w_spatial, preferred_element_type=jnp.float32).reshape(
        clip_latent.shape
    )
    hidden = jax.nn.silu(pre_act).astype(jnp.bfloat16)
    past_hidden = from_behind(hidden, "tm", 1)

    down = w_down.reshape(3, chans, chans)
    flipped_temporal = flip_blocks(w_temporal, 3)
    flipped_spatial = flip_blocks(w_spatial, 9)
    ahead_grad = jnp.concatenate([grad_out, next_grad, later_grad], axis=1)
    even_weight = jnp.concatenate([down[2], down[0]], axis=1)
    even_columns = jnp.concatenate([ahead_grad[:, 0:2], ahead_grad[:, 1:3]], axis=-1)

    def times_transpose(left, weight):
        return lax.dot_general(
            left, weight, (((4,), (1,)), ((), ())), preferred_element_type=jnp.float32
        ).astype(jnp.bfloat16)

    even = times_transpose(even_columns, even_weight)
    odd = times_transpose(ahead_grad[:, 1:3], down[1])
    extended_dy = jnp.concatenate([even[:, 0:1], odd[:, 0:1], even[:, 1:2], odd[:, 1:2]], axis=1)
    mixed_grad = extended_dy[:, 0:2]
    columns_dy = frame_columns(extended_dy, frames, (2, 1, 0))
    hidden_grad = jnp.dot(columns_dy, flipped_temporal, preferred_element_type=jnp.float32).reshape(
        clip_latent.shape
    )
    sigma = jax.nn.sigmoid(pre_act)
    act_grad = (hidden_grad * sigma * (1.0 + pre_act * (1.0 - sigma))).astype(jnp.bfloat16)
    rim_grad = padded_2(act_grad, (("space", 2),), 1)

    temporal_sum = causal_mix(past_hidden, hidden, w_temporal)
    mixed = (clip_latent.astype(jnp.float32) + temporal_sum).astype(jnp.bfloat16)

    def contract(left, right):
        return lax.dot_general(
            merge_cells(left),
            merge_cells(right),
            (((0,), (0,)), ((), ())),
            preferred_element_type=jnp.float32,
        ).astype(jnp.bfloat16)

    spatial_part = contract(columns_x, act_grad)
    temporal_part = jnp.concatenate(
        [contract(hidden, extended_dy[:, 2 - k : 4 - k]) for k in range(3)], axis=0
    )
    down_part = jnp.concatenate(
        [
            contract(mixed[:, 0:1], next_grad),
            contract(mixed[:, 1:2], next_grad),
            contract(mixed[:, 0:1], grad_out),
        ],
        axis=0,
    )
    pieces = [
        part.reshape(cores, groups, -1, chans) for part in (spatial_part, temporal_part, down_part)
    ]
    sizes = [piece.shape[2] for piece in pieces]
    fill = -sum(sizes) % 16
    if fill:
        pieces.append(jnp.zeros((cores, groups, fill, chans), jnp.bfloat16))
    reduced = reduce_parts(jnp.concatenate(pieces, axis=2), scale)
    grad_spatial = reduced[:, : sizes[0]]
    grad_temporal = reduced[:, sizes[0] : sizes[0] + sizes[1]]
    grad_down = reduced[:, sizes[0] + sizes[1] : sum(sizes)]

    columns_da = spatial_columns(pad_columns(rim_grad), rows, cols, True)
    spread_back = jnp.dot(columns_da, flipped_spatial, preferred_element_type=jnp.float32).reshape(
        clip_latent.shape
    )
    latent_grad = (mixed_grad.astype(jnp.float32) + spread_back).astype(jnp.bfloat16)
    return (latent_grad, grad_spatial, grad_temporal, grad_down)


def solution(mesh):
    placed = (P("dp", "tm", "space", None, None), P("dp", "tm", "space", None, None), P(), P(), P())
    return jax.shard_map(
        per_device,
        mesh=mesh,
        in_specs=placed,
        out_specs=(
            P("dp", "tm", "space", None, None),
            P("space", ("dp", "tm")),
            P("space", ("dp", "tm")),
            P("space", ("dp", "tm")),
        ),
        check_vma=False,
    )
```

```python
import functools
import math

import jax
import jax.numpy as jnp
from jax import lax
from jax.experimental import pallas as pl
from jax.experimental.pallas import tpu as pltpu
from jax.sharding import PartitionSpec as P

F32 = jnp.float32
BF16 = jnp.bfloat16


def round_up(size, step):
    return (size + step - 1) // step * step


def dot_nn(left, right):
    return jnp.dot(left, right, preferred_element_type=F32)


def dot_nt(left, right):
    return lax.dot_general(left, right, (((1,), (1,)), ((), ())), preferred_element_type=F32)


def dot_tn(left, right):
    return lax.dot_general(left, right, (((0,), (0,)), ((), ())), preferred_element_type=F32)


def block_kernel(
    groups,
    bands,
    cols,
    scale,
    x_ref,
    go_ref,
    ws_ref,
    wt_ref,
    wd_ref,
    latent_ref,
    out_ref,
    x_pad,
    x_shift,
    a_pad,
    a_shift,
    pre,
    hid,
    ahead,
    dy,
    parts,
    outgoing,
    from_core,
    mid,
    from_group,
    total,
    turned,
    turned_wide,
    from_band,
    edge_send,
    edge_recv,
    core_send,
    core_recv,
    group_send,
    group_recv,
    band_send,
    band_recv,
):
    core = lax.axis_index("dp")
    group = lax.axis_index("tm")
    band = lax.axis_index("space")
    chans = x_ref.shape[2]
    cells = x_ref.shape[1]
    rows = parts.shape[2]
    share = (9 * chans // (2 * groups), 3 * chans // (2 * groups), 3 * chans // (2 * groups))
    first = (0, share[0], share[0] + share[1])

    def at(d, t, s):
        return dict(device_id=(d, t, s), device_id_type=pl.DeviceIdType.MESH)

    barrier = pltpu.get_barrier_semaphore()
    pl.semaphore_signal(barrier, inc=1, **at(1 - core, group, band))
    for i in range(groups - 1):
        pl.semaphore_signal(barrier, inc=1, **at(core, lax.rem(group + 1 + i, groups), band))
    for i in range(bands - 1):
        pl.semaphore_signal(barrier, inc=1, **at(core, group, lax.rem(band + 1 + i, bands)))
    pl.semaphore_wait(barrier, groups + bands - 1)

    def make(n, src, dst, where):
        return pltpu.make_async_remote_copy(
            src_ref=src,
            dst_ref=dst,
            send_sem=edge_send.at[n],
            recv_sem=edge_recv.at[n],
            **where,
        )

    below = lax.rem(band + 1, bands)
    above = lax.rem(band + bands - 1, bands)
    before = lax.rem(group + groups - 1, groups)
    before2 = lax.rem(group + groups - 2, groups)
    after = lax.rem(group + 1, groups)
    low = pl.ds(0, cols)
    high = pl.ds(cells + cols, cols)
    moves = (
        (
            lambda: make(0, x_ref.at[:, pl.ds(cells - cols, cols)], x_pad.at[:, low], at(core, group, below)),
            band < bands - 1,
            band > 0,
        ),
        (
            lambda: make(1, x_ref.at[:, pl.ds(0, cols)], x_pad.at[:, high], at(core, group, above)),
            band > 0,
            band < bands - 1,
        ),
        (
            lambda: make(2, go_ref, ahead.at[0], at(core, before, band)),
            group > 0,
            group < groups - 1,
        ),
        (
            lambda: make(3, go_ref, ahead.at[1], at(core, before2, band)),
            group > 1,
            group < groups - 2,
        ),
        (
            lambda: make(4, hid.at[pl.ds(2, 2)], hid.at[pl.ds(0, 2)], at(core, after, band)),
            group < groups - 1,
            group > 0,
        ),
        (
            lambda: make(5, a_pad.at[:, pl.ds(cells, cols)], a_pad.at[:, low], at(core, group, below)),
            band < bands - 1,
            band > 0,
        ),
        (
            lambda: make(6, a_pad.at[:, pl.ds(cols, cols)], a_pad.at[:, high], at(core, group, above)),
            band > 0,
            band < bands - 1,
        ),
    )

    def start(n):
        @pl.when(moves[n][1])
        def _():
            moves[n][0]().start()

    def arrive(n):
        @pl.when(moves[n][2])
        def _():
            moves[n][0]().wait_recv()

    def sent(n):
        @pl.when(moves[n][1])
        def _():
            moves[n][0]().wait_send()

    for n in range(4):
        start(n)

    edge_zero = jnp.zeros((2, cols, chans), BF16)

    @pl.when(band == 0)
    def _():
        x_pad[:, 0:cols] = edge_zero
        a_pad[:, 0:cols] = edge_zero

    @pl.when(band == bands - 1)
    def _():
        x_pad[:, cells + cols : cells + 2 * cols] = edge_zero
        a_pad[:, cells + cols : cells + 2 * cols] = edge_zero

    @pl.when(group == groups - 1)
    def _():
        ahead[0] = jnp.zeros((cells, chans), BF16)

    @pl.when(group >= groups - 2)
    def _():
        ahead[1] = jnp.zeros((cells, chans), BF16)

    @pl.when(group == 0)
    def _():
        hid[0:2] = jnp.zeros((2, cells, chans), BF16)

    def shift(source, target, order):
        length = cells + 2 * cols
        place = lax.rem(lax.broadcasted_iota(jnp.int32, (length, chans), 0), cols)
        for f in range(2):
            plain = source[f]
            wide = plain.astype(F32)
            left = jnp.where(place == 0, 0.0, pltpu.roll(wide, 1, 0)).astype(BF16)
            right = jnp.where(place == cols - 1, 0.0, pltpu.roll(wide, length - 1, 0)).astype(BF16)
            values = (left, plain, right)
            for j in range(3):
                target[f, :, j * chans : (j + 1) * chans] = values[order[j]]

    x_pad[:, cols : cells + cols] = x_ref[...]
    arrive(0)
    arrive(1)
    shift(x_pad, x_shift, (0, 1, 2))
    for f in range(2):
        acc = jnp.zeros((cells, chans), F32)
        for i in range(3):
            acc += dot_nn(
                x_shift[f, i * cols : i * cols + cells, :],
                ws_ref[3 * i * chans : 3 * (i + 1) * chans, :],
            )
        pre[f] = acc
        hid[2 + f] = (acc / (1.0 + jnp.exp(-acc))).astype(BF16)
    start(4)

    arrive(2)
    arrive(3)

    def down(k):
        return wd_ref[k * chans : (k + 1) * chans, :]

    def temporal(k):
        return wt_ref[k * chans : (k + 1) * chans, :]

    dy[0] = (dot_nt(go_ref[...], down(2)) + dot_nt(ahead[0], down(0))).astype(BF16)
    dy[1] = dot_nt(ahead[0], down(1)).astype(BF16)
    dy[2] = (dot_nt(ahead[0], down(2)) + dot_nt(ahead[1], down(0))).astype(BF16)
    dy[3] = dot_nt(ahead[1], down(1)).astype(BF16)
    for f in range(2):
        back = jnp.zeros((cells, chans), F32)
        for k in range(3):
            back += dot_nt(dy[f + 2 - k], temporal(k))
        value = pre[f]
        gate = 1.0 / (1.0 + jnp.exp(-value))
        a_pad[f, cols : cells + cols] = (back * gate * (1.0 + value * (1.0 - gate))).astype(BF16)
    start(5)
    start(6)

    def put(kind, begin, values):
        done = 0
        size = values.shape[0]
        while done < size:
            spot = begin + done
            owner, inner = spot // share[kind], spot % share[kind]
            count = min(share[kind] - inner, size - done)
            offset = first[kind] + inner
            parts[owner // groups, owner % groups, offset : offset + count, :] = values[
                done : done + count
            ]
            done += count

    if rows > sum(share):
        for d in range(2):
            for t in range(groups):
                parts[d, t, sum(share) :, :] = jnp.zeros((rows - sum(share), chans), F32)

    for i in range(3):
        for j in range(3):
            acc = jnp.zeros((chans, chans), F32)
            for f in range(2):
                acc += dot_tn(
                    x_shift[f, i * cols : i * cols + cells, j * chans : (j + 1) * chans],
                    a_pad[f, cols : cells + cols, :],
                )
            put(0, (3 * i + j) * chans, acc)
    for k in range(3):
        put(1, k * chans, dot_tn(hid[2], dy[2 - k]) + dot_tn(hid[3], dy[3 - k]))

    arrive(4)
    mixed = []
    for f in range(2):
        acc = x_ref[f].astype(F32)
        acc += (
            dot_nn(hid[f], temporal(0))
            + dot_nn(hid[f + 1], temporal(1))
            + dot_nn(hid[f + 2], temporal(2))
        )
        mixed.append(acc.astype(BF16))
    put(2, 0, dot_tn(mixed[0], ahead[0]))
    put(2, chans, dot_tn(mixed[1], ahead[0]))
    put(2, 2 * chans, dot_tn(mixed[0], go_ref[...]))

    core_copies = []
    for i in range(groups):
        target = lax.rem(group + 1 + i, groups)
        outgoing[i] = parts[1 - core, target].astype(BF16)
        copy = pltpu.make_async_remote_copy(
            src_ref=outgoing.at[i],
            dst_ref=from_core.at[i],
            send_sem=core_send.at[i],
            recv_sem=core_recv.at[i],
            **at(1 - core, group, band),
        )
        copy.start()
        core_copies.append(copy)

    group_copies = []
    for i in range(groups):
        target = lax.rem(group + 1 + i, groups)
        core_copies[i].wait_recv()
        summed = parts[core, target] + from_core[i].astype(F32)
        if i == groups - 1:
            total[0:rows, :] = summed
        else:
            mid[i] = summed.astype(BF16)
            copy = pltpu.make_async_remote_copy(
                src_ref=mid.at[i],
                dst_ref=from_group.at[i],
                send_sem=group_send.at[i],
                recv_sem=group_recv.at[i],
                **at(core, target, band),
            )
            copy.start()
            group_copies.append(copy)
    if total.shape[0] > rows:
        total[rows:, :] = jnp.zeros((total.shape[0] - rows, chans), F32)

    arrive(5)
    arrive(6)
    shift(a_pad, a_shift, (2, 1, 0))
    for f in range(2):
        acc = dy[f].astype(F32)
        for i in range(3):
            for j in range(3):
                tap = 3 * i + j
                acc += dot_nt(
                    a_shift[f, (2 - i) * cols : (2 - i) * cols + cells, j * chans : (j + 1) * chans],
                    ws_ref[tap * chans : (tap + 1) * chans, :],
                )
        latent_ref[f] = acc.astype(BF16)

    for i in range(groups - 1):
        group_copies[i].wait_recv()
        total[0:rows, :] += from_group[i].astype(F32)

    flat = (total[...] * scale).T.reshape(turned.shape)
    turned_wide[...] = flat
    turned[...] = flat.astype(BF16)
    band_copies = []
    for i in range(bands - 1):
        target = lax.rem(band + 1 + i, bands)
        copy = pltpu.make_async_remote_copy(
            src_ref=turned.at[target],
            dst_ref=from_band.at[i],
            send_sem=band_send.at[i],
            recv_sem=band_recv.at[i],
            **at(core, group, target),
        )
        copy.start()
        band_copies.append(copy)
    result = turned_wide[band]
    for i in range(bands - 1):
        band_copies[i].wait_recv()
        result += from_band[i].astype(F32)
    out_ref[...] = result
    for n in range(7):
        sent(n)
    for copy in core_copies + group_copies + band_copies:
        copy.wait_send()


def per_device(clip_latent, grad_out, w_spatial, w_temporal, w_down):
    clips, frames, height, cols, chans = clip_latent.shape
    groups = lax.axis_size("tm")
    bands = lax.axis_size("space")
    assert clips == 1 and frames == 2 and grad_out.shape[1] == 1 and lax.axis_size("dp") == 2
    count = clips * frames * height * cols * 2 * groups * bands
    scale = 1.0 / math.sqrt(count)
    cells = height * cols
    padded = cells + 2 * cols
    sizes = (9 * chans // (2 * groups), 3 * chans // (2 * groups), 3 * chans // (2 * groups))
    rows = round_up(sum(sizes), 16)
    wide = round_up(rows, 128)
    share = chans // bands
    dma = pltpu.SemaphoreType.DMA
    vmem = pl.BlockSpec(memory_space=pltpu.VMEM)
    latent, reduced = pl.pallas_call(
        functools.partial(block_kernel, groups, bands, cols, scale),
        out_shape=(
            jax.ShapeDtypeStruct((2, cells, chans), BF16),
            jax.ShapeDtypeStruct((share, wide), F32),
        ),
        in_specs=[vmem] * 5,
        out_specs=(vmem, vmem),
        scratch_shapes=[
            pltpu.VMEM((2, padded, chans), BF16),
            pltpu.VMEM((2, padded, 3 * chans), BF16),
            pltpu.VMEM((2, padded, chans), BF16),
            pltpu.VMEM((2, padded, 3 * chans), BF16),
            pltpu.VMEM((2, cells, chans), F32),
            pltpu.VMEM((4, cells, chans), BF16),
            pltpu.VMEM((2, cells, chans), BF16),
            pltpu.VMEM((4, cells, chans), BF16),
            pltpu.VMEM((2, groups, rows, chans), F32),
            pltpu.VMEM((groups, rows, chans), BF16),
            pltpu.VMEM((groups, rows, chans), BF16),
            pltpu.VMEM((groups - 1, rows, chans), BF16),
            pltpu.VMEM((groups - 1, rows, chans), BF16),
            pltpu.VMEM((wide, chans), F32),
            pltpu.VMEM((bands, share, wide), BF16),
            pltpu.VMEM((bands, share, wide), F32),
            pltpu.VMEM((bands - 1, share, wide), BF16),
            dma((7,)),
            dma((7,)),
            dma((groups,)),
            dma((groups,)),
            dma((groups - 1,)),
            dma((groups - 1,)),
            dma((bands - 1,)),
            dma((bands - 1,)),
        ],
        compiler_params=pltpu.CompilerParams(
            collective_id=0, has_side_effects=True, vmem_limit_bytes=50 * 1024 * 1024
        ),
    )(
        clip_latent.reshape(2, cells, chans),
        grad_out.reshape(cells, chans),
        w_spatial,
        w_temporal,
        w_down,
    )
    return (
        latent.reshape(clip_latent.shape),
        reduced[:, : sizes[0]],
        reduced[:, sizes[0] : sizes[0] + sizes[1]],
        reduced[:, sizes[0] + sizes[1] : sum(sizes)],
    )


def solution(mesh):
    placed = (P("dp", "tm", "space", None, None), P("dp", "tm", "space", None, None), P(), P(), P())
    return jax.shard_map(
        per_device,
        mesh=mesh,
        in_specs=placed,
        out_specs=(
            P("dp", "tm", "space", None, None),
            P("space", ("dp", "tm")),
            P("space", ("dp", "tm")),
            P("space", ("dp", "tm")),
        ),
        check_vma=False,
    )
```

```python
import functools
import math

import jax
import jax.numpy as jnp
from jax import lax
from jax.experimental import pallas as pl
from jax.experimental.pallas import tpu as pltpu
from jax.sharding import PartitionSpec as P

F32 = jnp.float32
BF16 = jnp.bfloat16


def round_up(size, step):
    return (size + step - 1) // step * step


def dot_nn(left, right):
    return jnp.dot(left, right, preferred_element_type=F32)


def dot_nt(left, right):
    return lax.dot_general(left, right, (((1,), (1,)), ((), ())), preferred_element_type=F32)


def dot_tn(left, right):
    return lax.dot_general(left, right, (((0,), (0,)), ((), ())), preferred_element_type=F32)


def block_kernel(
    groups,
    bands,
    cols,
    scale,
    x_far,
    go_far,
    ws_far,
    wt_far,
    wd_far,
    latent_ref,
    out_ref,
    out_late,
    x_ref,
    go_ref,
    ws_ref,
    wt_ref,
    wd_ref,
    load_sem,
    x_pad,
    x_shift,
    a_pad,
    a_shift,
    pre,
    hid,
    ahead,
    dy,
    parts_0,
    parts_1,
    outgoing_0,
    outgoing_1,
    from_core_0,
    from_core_1,
    mid_0,
    mid_1,
    from_group_0,
    from_group_1,
    total_0,
    total_1,
    turned_0,
    turned_1,
    turned_wide_0,
    turned_wide_1,
    from_band_0,
    from_band_1,
    edge_send,
    edge_recv,
    core_send,
    core_recv,
    group_send,
    group_recv,
    band_send,
    band_recv,
):
    core = lax.axis_index("dp")
    group = lax.axis_index("tm")
    band = lax.axis_index("space")
    chans = x_ref.shape[2]
    cells = x_ref.shape[1]
    share = (9 * chans // (2 * groups), 3 * chans // (2 * groups), 3 * chans // (2 * groups))
    first = (0, 0, share[1])
    phase = (0, 1, 1)
    loads = [
        pltpu.make_async_copy(src, dst, load_sem.at[n])
        for n, (src, dst) in enumerate(
            (
                (x_far, x_ref),
                (ws_far, ws_ref),
                (go_far, go_ref),
                (wd_far, wd_ref),
                (wt_far, wt_ref),
            )
        )
    ]
    for load in loads:
        load.start()

    def at(d, t, s):
        return dict(device_id=(d, t, s), device_id_type=pl.DeviceIdType.MESH)

    barrier = pltpu.get_barrier_semaphore()
    pl.semaphore_signal(barrier, inc=1, **at(1 - core, group, band))
    for i in range(groups - 1):
        pl.semaphore_signal(barrier, inc=1, **at(core, lax.rem(group + 1 + i, groups), band))
    for i in range(bands - 1):
        pl.semaphore_signal(barrier, inc=1, **at(core, group, lax.rem(band + 1 + i, bands)))
    pl.semaphore_wait(barrier, groups + bands - 1)

    def make(n, src, dst, where):
        return pltpu.make_async_remote_copy(
            src_ref=src,
            dst_ref=dst,
            send_sem=edge_send.at[n],
            recv_sem=edge_recv.at[n],
            **where,
        )

    below = lax.rem(band + 1, bands)
    above = lax.rem(band + bands - 1, bands)
    before = lax.rem(group + groups - 1, groups)
    before2 = lax.rem(group + groups - 2, groups)
    after = lax.rem(group + 1, groups)
    low = pl.ds(0, cols)
    high = pl.ds(cells + cols, cols)
    moves = (
        (
            lambda: make(0, x_far.at[:, pl.ds(cells - cols, cols)], x_pad.at[:, low], at(core, group, below)),
            band < bands - 1,
            band > 0,
        ),
        (
            lambda: make(1, x_far.at[:, pl.ds(0, cols)], x_pad.at[:, high], at(core, group, above)),
            band > 0,
            band < bands - 1,
        ),
        (
            lambda: make(2, go_far, ahead.at[0], at(core, before, band)),
            group > 0,
            group < groups - 1,
        ),
        (
            lambda: make(3, go_far, ahead.at[1], at(core, before2, band)),
            group > 1,
            group < groups - 2,
        ),
        (
            lambda: make(4, a_pad.at[:, pl.ds(cells, cols)], a_pad.at[:, low], at(core, group, below)),
            band < bands - 1,
            band > 0,
        ),
        (
            lambda: make(5, a_pad.at[:, pl.ds(cols, cols)], a_pad.at[:, high], at(core, group, above)),
            band > 0,
            band < bands - 1,
        ),
    )

    def start(n):
        @pl.when(moves[n][1])
        def _():
            moves[n][0]().start()

    def arrive(n):
        @pl.when(moves[n][2])
        def _():
            moves[n][0]().wait_recv()

    def sent(n):
        @pl.when(moves[n][1])
        def _():
            moves[n][0]().wait_send()

    for n in range(4):
        start(n)

    edge_zero = jnp.zeros((2, cols, chans), BF16)

    @pl.when(band == 0)
    def _():
        x_pad[:, 0:cols] = edge_zero
        a_pad[:, 0:cols] = edge_zero

    @pl.when(band == bands - 1)
    def _():
        x_pad[:, cells + cols : cells + 2 * cols] = edge_zero
        a_pad[:, cells + cols : cells + 2 * cols] = edge_zero

    @pl.when(group == groups - 1)
    def _():
        ahead[0] = jnp.zeros((cells, chans), BF16)

    @pl.when(group >= groups - 2)
    def _():
        ahead[1] = jnp.zeros((cells, chans), BF16)

    def shift(source, target, order):
        length = cells + 2 * cols
        place = lax.rem(lax.broadcasted_iota(jnp.int32, (length, chans), 0), cols)
        for f in range(2):
            plain = source[f]
            wide = plain.astype(F32)
            left = jnp.where(place == 0, 0.0, pltpu.roll(wide, 1, 0)).astype(BF16)
            right = jnp.where(place == cols - 1, 0.0, pltpu.roll(wide, length - 1, 0)).astype(BF16)
            values = (left, plain, right)
            for j in range(3):
                target[f, :, j * chans : (j + 1) * chans] = values[order[j]]

    loads[0].wait()
    x_pad[:, cols : cells + cols] = x_ref[...]
    arrive(0)
    arrive(1)
    shift(x_pad, x_shift, (0, 1, 2))
    loads[1].wait()
    for f in range(2):
        acc = jnp.zeros((cells, chans), F32)
        for i in range(3):
            acc += dot_nn(
                x_shift[f, i * cols : i * cols + cells, :],
                ws_ref[3 * i * chans : 3 * (i + 1) * chans, :],
            )
        pre[f] = acc
        hid[f] = (acc / (1.0 + jnp.exp(-acc))).astype(BF16)
    arrive(2)
    arrive(3)
    for load in loads[2:]:
        load.wait()

    def down(k):
        return wd_ref[k * chans : (k + 1) * chans, :]

    def temporal(k):
        return wt_ref[k * chans : (k + 1) * chans, :]

    dy[0] = (dot_nt(go_ref[...], down(2)) + dot_nt(ahead[0], down(0))).astype(BF16)
    dy[1] = dot_nt(ahead[0], down(1)).astype(BF16)
    dy[2] = (dot_nt(ahead[0], down(2)) + dot_nt(ahead[1], down(0))).astype(BF16)
    dy[3] = dot_nt(ahead[1], down(1)).astype(BF16)
    both = (
        (parts_0, outgoing_0, from_core_0, mid_0, from_group_0, total_0),
        (parts_1, outgoing_1, from_core_1, mid_1, from_group_1, total_1),
    )

    def put(kind, begin, values):
        done = 0
        size = values.shape[0]
        while done < size:
            spot = begin + done
            owner, inner = spot // share[kind], spot % share[kind]
            count = min(share[kind] - inner, size - done)
            offset = first[kind] + inner
            both[phase[kind]][0][owner // groups, owner % groups, offset : offset + count, :] = values[
                done : done + count
            ]
            done += count

    for held, used in ((parts_0, share[0]), (parts_1, share[1] + share[2])):
        if held.shape[2] > used:
            for d in range(2):
                for t in range(groups):
                    held[d, t, used:, :] = jnp.zeros((held.shape[2] - used, chans), F32)

    core_copies = ([], [])
    group_copies = ([], [])
    band_copies = ([], [])

    def give_core(p):
        parts, outgoing, from_core = both[p][:3]
        for i in range(groups):
            target = lax.rem(group + 1 + i, groups)
            outgoing[i] = parts[1 - core, target].astype(BF16)
            copy = pltpu.make_async_remote_copy(
                src_ref=outgoing.at[i],
                dst_ref=from_core.at[i],
                send_sem=core_send.at[p, i],
                recv_sem=core_recv.at[p, i],
                **at(1 - core, group, band),
            )
            copy.start()
            core_copies[p].append(copy)

    def give_group(p):
        parts, _, from_core, mid, from_group, total = both[p]
        rows = parts.shape[2]
        for i in range(groups):
            target = lax.rem(group + 1 + i, groups)
            core_copies[p][i].wait_recv()
            summed = parts[core, target] + from_core[i].astype(F32)
            if i == groups - 1:
                total[0:rows, :] = summed
            else:
                mid[i] = summed.astype(BF16)
                copy = pltpu.make_async_remote_copy(
                    src_ref=mid.at[i],
                    dst_ref=from_group.at[i],
                    send_sem=group_send.at[p, i],
                    recv_sem=group_recv.at[p, i],
                    **at(core, target, band),
                )
                copy.start()
                group_copies[p].append(copy)
        if total.shape[0] > rows:
            total[rows:, :] = jnp.zeros((total.shape[0] - rows, chans), F32)

    last = (
        (turned_0, turned_wide_0, from_band_0, out_ref),
        (turned_1, turned_wide_1, from_band_1, out_late),
    )

    def give_band(p):
        from_group, total = both[p][4:]
        turned, turned_wide, from_band, _ = last[p]
        rows = from_group.shape[1]
        for i in range(groups - 1):
            group_copies[p][i].wait_recv()
            total[0:rows, :] += from_group[i].astype(F32)
        flat = (total[...] * scale).T.reshape(turned.shape)
        turned_wide[...] = flat
        turned[...] = flat.astype(BF16)
        for i in range(bands - 1):
            target = lax.rem(band + 1 + i, bands)
            copy = pltpu.make_async_remote_copy(
                src_ref=turned.at[target],
                dst_ref=from_band.at[i],
                send_sem=band_send.at[p, i],
                recv_sem=band_recv.at[p, i],
                **at(core, group, target),
            )
            copy.start()
            band_copies[p].append(copy)

    def finish(p):
        _, turned_wide, from_band, result_ref = last[p]
        result = turned_wide[band]
        for i in range(bands - 1):
            band_copies[p][i].wait_recv()
            result += from_band[i].astype(F32)
        result_ref[...] = result

    for k in range(3):
        put(1, k * chans, dot_tn(hid[0], dy[2 - k]) + dot_tn(hid[1], dy[3 - k]))
    pairs = (
        dot_tn(hid[0], ahead[1]),
        dot_tn(hid[1], ahead[1]),
        dot_tn(hid[0], ahead[0]),
        dot_tn(hid[1], ahead[0]),
        dot_tn(hid[0], go_ref[...]),
    )
    coarse = [pair.astype(BF16) for pair in pairs]
    fine = [(pair - part.astype(F32)).astype(BF16) for pair, part in zip(pairs, coarse)]
    direct = (
        dot_tn(x_ref[0], ahead[0]),
        dot_tn(x_ref[1], ahead[0]),
        dot_tn(x_ref[0], go_ref[...]),
    )
    for k in range(3):
        acc = direct[k]
        for n in range(3):
            acc += dot_tn(temporal(n), coarse[k + n]) + dot_tn(temporal(n), fine[k + n])
        put(2, k * chans, acc)
    give_core(1)
    for f in range(2):
        back = jnp.zeros((cells, chans), F32)
        for k in range(3):
            back += dot_nt(dy[f + 2 - k], temporal(k))
        value = pre[f]
        gate = 1.0 / (1.0 + jnp.exp(-value))
        a_pad[f, cols : cells + cols] = (back * gate * (1.0 + value * (1.0 - gate))).astype(BF16)
    start(4)
    start(5)

    give_group(1)
    for i in range(3):
        for j in range(3):
            acc = jnp.zeros((chans, chans), F32)
            for f in range(2):
                acc += dot_tn(
                    x_shift[f, i * cols : i * cols + cells, j * chans : (j + 1) * chans],
                    a_pad[f, cols : cells + cols, :],
                )
            put(0, (3 * i + j) * chans, acc)
    give_core(0)
    give_band(1)
    give_group(0)
    arrive(4)
    arrive(5)
    shift(a_pad, a_shift, (2, 1, 0))
    for f in range(2):
        acc = dy[f].astype(F32)
        for i in range(3):
            for j in range(3):
                tap = 3 * i + j
                acc += dot_nt(
                    a_shift[f, (2 - i) * cols : (2 - i) * cols + cells, j * chans : (j + 1) * chans],
                    ws_ref[tap * chans : (tap + 1) * chans, :],
                )
        latent_ref[f] = acc.astype(BF16)

    give_band(0)
    finish(1)
    finish(0)
    for n in range(6):
        sent(n)
    for p in range(2):
        for copy in core_copies[p] + group_copies[p] + band_copies[p]:
            copy.wait_send()


def per_device(clip_latent, grad_out, w_spatial, w_temporal, w_down):
    clips, frames, height, cols, chans = clip_latent.shape
    groups = lax.axis_size("tm")
    bands = lax.axis_size("space")
    assert clips == 1 and frames == 2 and grad_out.shape[1] == 1 and lax.axis_size("dp") == 2
    count = clips * frames * height * cols * 2 * groups * bands
    scale = 1.0 / math.sqrt(count)
    cells = height * cols
    padded = cells + 2 * cols
    sizes = (9 * chans // (2 * groups), 3 * chans // (2 * groups), 3 * chans // (2 * groups))
    rows = (round_up(sizes[0], 16), round_up(sizes[1] + sizes[2], 16))
    wide = tuple(round_up(size, 128) for size in rows)
    share = chans // bands
    dma = pltpu.SemaphoreType.DMA
    vmem = pl.BlockSpec(memory_space=pltpu.VMEM)
    latent, spatial, others = pl.pallas_call(
        functools.partial(block_kernel, groups, bands, cols, scale),
        out_shape=(
            jax.ShapeDtypeStruct((2, cells, chans), BF16),
            jax.ShapeDtypeStruct((share, wide[0]), F32),
            jax.ShapeDtypeStruct((share, wide[1]), F32),
        ),
        in_specs=[pl.BlockSpec(memory_space=pl.ANY)] * 5,
        out_specs=(vmem, vmem, vmem),
        scratch_shapes=[
            pltpu.VMEM((2, cells, chans), BF16),
            pltpu.VMEM((cells, chans), BF16),
            pltpu.VMEM(w_spatial.shape, BF16),
            pltpu.VMEM(w_temporal.shape, BF16),
            pltpu.VMEM(w_down.shape, BF16),
            dma((5,)),
            pltpu.VMEM((2, padded, chans), BF16),
            pltpu.VMEM((2, padded, 3 * chans), BF16),
            pltpu.VMEM((2, padded, chans), BF16),
            pltpu.VMEM((2, padded, 3 * chans), BF16),
            pltpu.VMEM((2, cells, chans), F32),
            pltpu.VMEM((2, cells, chans), BF16),
            pltpu.VMEM((2, cells, chans), BF16),
            pltpu.VMEM((4, cells, chans), BF16),
            pltpu.VMEM((2, groups, rows[0], chans), F32),
            pltpu.VMEM((2, groups, rows[1], chans), F32),
            pltpu.VMEM((groups, rows[0], chans), BF16),
            pltpu.VMEM((groups, rows[1], chans), BF16),
            pltpu.VMEM((groups, rows[0], chans), BF16),
            pltpu.VMEM((groups, rows[1], chans), BF16),
            pltpu.VMEM((groups - 1, rows[0], chans), BF16),
            pltpu.VMEM((groups - 1, rows[1], chans), BF16),
            pltpu.VMEM((groups - 1, rows[0], chans), BF16),
            pltpu.VMEM((groups - 1, rows[1], chans), BF16),
            pltpu.VMEM((wide[0], chans), F32),
            pltpu.VMEM((wide[1], chans), F32),
            pltpu.VMEM((bands, share, wide[0]), BF16),
            pltpu.VMEM((bands, share, wide[1]), BF16),
            pltpu.VMEM((bands, share, wide[0]), F32),
            pltpu.VMEM((bands, share, wide[1]), F32),
            pltpu.VMEM((bands - 1, share, wide[0]), BF16),
            pltpu.VMEM((bands - 1, share, wide[1]), BF16),
            dma((6,)),
            dma((6,)),
            dma((2, groups)),
            dma((2, groups)),
            dma((2, groups - 1)),
            dma((2, groups - 1)),
            dma((2, bands - 1)),
            dma((2, bands - 1)),
        ],
        compiler_params=pltpu.CompilerParams(
            collective_id=0, has_side_effects=True, vmem_limit_bytes=58 * 1024 * 1024
        ),
    )(
        clip_latent.reshape(2, cells, chans),
        grad_out.reshape(cells, chans),
        w_spatial,
        w_temporal,
        w_down,
    )
    return (
        latent.reshape(clip_latent.shape),
        spatial[:, : sizes[0]],
        others[:, : sizes[1]],
        others[:, sizes[1] : sizes[1] + sizes[2]],
    )


def solution(mesh):
    placed = (P("dp", "tm", "space", None, None), P("dp", "tm", "space", None, None), P(), P(), P())
    return jax.shard_map(
        per_device,
        mesh=mesh,
        in_specs=placed,
        out_specs=(
            P("dp", "tm", "space", None, None),
            P("space", ("dp", "tm")),
            P("space", ("dp", "tm")),
            P("space", ("dp", "tm")),
        ),
        check_vma=False,
    )
```

```python
import functools
import math

import jax
import jax.numpy as jnp
from jax import lax
from jax.experimental import pallas as pl
from jax.experimental.pallas import tpu as pltpu
from jax.sharding import PartitionSpec as P

F32 = jnp.float32
BF16 = jnp.bfloat16


def round_up(size, step):
    return (size + step - 1) // step * step


def dot_nn(left, right):
    return jnp.dot(left, right, preferred_element_type=F32)


def dot_nt(left, right):
    return lax.dot_general(left, right, (((1,), (1,)), ((), ())), preferred_element_type=F32)


def dot_tn(left, right):
    return lax.dot_general(left, right, (((0,), (0,)), ((), ())), preferred_element_type=F32)


def block_kernel(
    groups,
    bands,
    cols,
    scale,
    x_far,
    go_far,
    ws_far,
    wt_far,
    wd_far,
    latent_ref,
    out_ref,
    out_temporal,
    out_down,
    x_ref,
    go_ref,
    ws_ref,
    wt_ref,
    wd_ref,
    load_sem,
    x_pad,
    x_shift,
    a_pad,
    a_shift,
    pre,
    hid,
    ahead,
    dy,
    parts_0,
    parts_1,
    outgoing_0,
    outgoing_1,
    from_core_0,
    from_core_1,
    mid_0,
    mid_1,
    from_group_0,
    from_group_1,
    total_0,
    total_1,
    turned_0,
    turned_1,
    turned_wide_0,
    turned_wide_1,
    from_band_0,
    from_band_1,
    edge_send,
    edge_recv,
    core_send,
    core_recv,
    group_send,
    group_recv,
    band_send,
    band_recv,
):
    core = lax.axis_index("dp")
    group = lax.axis_index("tm")
    band = lax.axis_index("space")
    chans = x_ref.shape[2]
    cells = x_ref.shape[1]
    share = (9 * chans // (2 * groups), 3 * chans // (2 * groups), 3 * chans // (2 * groups))
    first = (0, 0, share[1])
    phase = (0, 1, 1)
    loads = [
        pltpu.make_async_copy(src, dst, load_sem.at[n])
        for n, (src, dst) in enumerate(
            (
                (x_far, x_ref),
                (ws_far, ws_ref),
                (go_far, go_ref),
                (wd_far, wd_ref),
                (wt_far, wt_ref),
            )
        )
    ]
    for load in loads:
        load.start()

    def at(d, t, s):
        return dict(device_id=(d, t, s), device_id_type=pl.DeviceIdType.MESH)

    barrier = pltpu.get_barrier_semaphore()
    pl.semaphore_signal(barrier, inc=1, **at(1 - core, group, band))
    for i in range(groups - 1):
        pl.semaphore_signal(barrier, inc=1, **at(core, lax.rem(group + 1 + i, groups), band))
    for i in range(bands - 1):
        pl.semaphore_signal(barrier, inc=1, **at(core, group, lax.rem(band + 1 + i, bands)))
    pl.semaphore_wait(barrier, groups + bands - 1)

    def make(n, src, dst, where):
        return pltpu.make_async_remote_copy(
            src_ref=src,
            dst_ref=dst,
            send_sem=edge_send.at[n],
            recv_sem=edge_recv.at[n],
            **where,
        )

    below = lax.rem(band + 1, bands)
    above = lax.rem(band + bands - 1, bands)
    before = lax.rem(group + groups - 1, groups)
    before2 = lax.rem(group + groups - 2, groups)
    after = lax.rem(group + 1, groups)
    low = pl.ds(0, cols)
    high = pl.ds(cells + cols, cols)
    moves = (
        (
            lambda: make(0, x_far.at[:, pl.ds(cells - cols, cols)], x_pad.at[:, low], at(core, group, below)),
            band < bands - 1,
            band > 0,
        ),
        (
            lambda: make(1, x_far.at[:, pl.ds(0, cols)], x_pad.at[:, high], at(core, group, above)),
            band > 0,
            band < bands - 1,
        ),
        (
            lambda: make(2, go_far, ahead.at[0], at(core, before, band)),
            group > 0,
            group < groups - 1,
        ),
        (
            lambda: make(3, go_far, ahead.at[1], at(core, before2, band)),
            group > 1,
            group < groups - 2,
        ),
        (
            lambda: make(4, a_pad.at[:, pl.ds(cells, cols)], a_pad.at[:, low], at(core, group, below)),
            band < bands - 1,
            band > 0,
        ),
        (
            lambda: make(5, a_pad.at[:, pl.ds(cols, cols)], a_pad.at[:, high], at(core, group, above)),
            band > 0,
            band < bands - 1,
        ),
    )

    def start(n):
        @pl.when(moves[n][1])
        def _():
            moves[n][0]().start()

    def arrive(n):
        @pl.when(moves[n][2])
        def _():
            moves[n][0]().wait_recv()

    def sent(n):
        @pl.when(moves[n][1])
        def _():
            moves[n][0]().wait_send()

    for n in range(4):
        start(n)

    edge_zero = jnp.zeros((2, cols, chans), BF16)

    @pl.when(band == 0)
    def _():
        x_pad[:, 0:cols] = edge_zero
        a_pad[:, 0:cols] = edge_zero

    @pl.when(band == bands - 1)
    def _():
        x_pad[:, cells + cols : cells + 2 * cols] = edge_zero
        a_pad[:, cells + cols : cells + 2 * cols] = edge_zero

    @pl.when(group == groups - 1)
    def _():
        ahead[0] = jnp.zeros((cells, chans), BF16)

    @pl.when(group >= groups - 2)
    def _():
        ahead[1] = jnp.zeros((cells, chans), BF16)

    def shift(source, target, order):
        length = cells + 2 * cols
        place = lax.rem(lax.broadcasted_iota(jnp.int32, (length, chans), 0), cols)
        for f in range(2):
            plain = source[f]
            wide = plain.astype(F32)
            left = jnp.where(place == 0, 0.0, pltpu.roll(wide, 1, 0)).astype(BF16)
            right = jnp.where(place == cols - 1, 0.0, pltpu.roll(wide, length - 1, 0)).astype(BF16)
            values = (left, plain, right)
            for j in range(3):
                target[f, :, j * chans : (j + 1) * chans] = values[order[j]]

    loads[0].wait()
    x_pad[:, cols : cells + cols] = x_ref[...]
    arrive(0)
    arrive(1)
    shift(x_pad, x_shift, (0, 1, 2))
    loads[1].wait()
    for f in range(2):
        acc = jnp.zeros((cells, chans), F32)
        for i in range(3):
            acc += dot_nn(
                x_shift[f, i * cols : i * cols + cells, :],
                ws_ref[3 * i * chans : 3 * (i + 1) * chans, :],
            )
        pre[f] = acc
        hid[f] = (acc / (1.0 + jnp.exp(-acc))).astype(BF16)
    arrive(2)
    for load in loads[2:]:
        load.wait()

    def down(k):
        return wd_ref[k * chans : (k + 1) * chans, :]

    def temporal(k):
        return wt_ref[k * chans : (k + 1) * chans, :]

    dy[0] = (dot_nt(go_ref[...], down(2)) + dot_nt(ahead[0], down(0))).astype(BF16)
    dy[1] = dot_nt(ahead[0], down(1)).astype(BF16)
    both = (
        (parts_0, outgoing_0, from_core_0, mid_0, from_group_0, total_0),
        (parts_1, outgoing_1, from_core_1, mid_1, from_group_1, total_1),
    )

    def put(kind, begin, values):
        done = 0
        size = values.shape[0]
        while done < size:
            spot = begin + done
            owner, inner = spot // share[kind], spot % share[kind]
            count = min(share[kind] - inner, size - done)
            offset = first[kind] + inner
            both[phase[kind]][0][owner // groups, owner % groups, offset : offset + count, :] = values[
                done : done + count
            ]
            done += count

    for held, used in ((parts_0, share[0]), (parts_1, share[1] + share[2])):
        if held.shape[2] > used:
            for d in range(2):
                for t in range(groups):
                    held[d, t, used:, :] = jnp.zeros((held.shape[2] - used, chans), F32)

    core_copies = ([], [])
    group_copies = ([], [])
    band_copies = ([], [])

    def give_core(p):
        parts, outgoing, from_core = both[p][:3]
        for i in range(groups):
            target = lax.rem(group + 1 + i, groups)
            outgoing[i] = parts[1 - core, target].astype(BF16)
            copy = pltpu.make_async_remote_copy(
                src_ref=outgoing.at[i],
                dst_ref=from_core.at[i],
                send_sem=core_send.at[p, i],
                recv_sem=core_recv.at[p, i],
                **at(1 - core, group, band),
            )
            copy.start()
            core_copies[p].append(copy)

    def give_group(p):
        parts, _, from_core, mid, from_group, total = both[p]
        rows = parts.shape[2]
        for i in range(groups):
            target = lax.rem(group + 1 + i, groups)
            core_copies[p][i].wait_recv()
            summed = parts[core, target] + from_core[i].astype(F32)
            if i == groups - 1:
                total[0:rows, :] = summed
            else:
                mid[i] = summed.astype(BF16)
                copy = pltpu.make_async_remote_copy(
                    src_ref=mid.at[i],
                    dst_ref=from_group.at[i],
                    send_sem=group_send.at[p, i],
                    recv_sem=group_recv.at[p, i],
                    **at(core, target, band),
                )
                copy.start()
                group_copies[p].append(copy)
        if total.shape[0] > rows:
            total[rows:, :] = jnp.zeros((total.shape[0] - rows, chans), F32)

    last = (
        (turned_0, turned_wide_0, from_band_0, ((out_ref, 0, share[0]),)),
        (turned_1, turned_wide_1, from_band_1, ((out_temporal, 0, share[1]), (out_down, share[1], share[2]))),
    )

    def give_band(p):
        from_group, total = both[p][4:]
        turned, turned_wide, from_band, _ = last[p]
        rows = from_group.shape[1]
        for i in range(groups - 1):
            group_copies[p][i].wait_recv()
            total[0:rows, :] += from_group[i].astype(F32)
        flat = (total[...] * scale).T.reshape(turned.shape)
        turned_wide[...] = flat
        turned[...] = flat.astype(BF16)
        for i in range(bands - 1):
            target = lax.rem(band + 1 + i, bands)
            copy = pltpu.make_async_remote_copy(
                src_ref=turned.at[target],
                dst_ref=from_band.at[i],
                send_sem=band_send.at[p, i],
                recv_sem=band_recv.at[p, i],
                **at(core, group, target),
            )
            copy.start()
            band_copies[p].append(copy)

    def finish(p):
        _, turned_wide, from_band, results = last[p]
        result = turned_wide[band]
        for i in range(bands - 1):
            band_copies[p][i].wait_recv()
            result += from_band[i].astype(F32)
        for result_ref, begin, size in results:
            result_ref[...] = result[:, begin : begin + size]

    put(1, 2 * chans, dot_tn(hid[0], dy[0]) + dot_tn(hid[1], dy[1]))
    near_pairs = (
        dot_tn(hid[0], ahead[0]),
        dot_tn(hid[1], ahead[0]),
        dot_tn(hid[0], go_ref[...]),
    )
    direct = (
        dot_tn(x_ref[0], ahead[0]),
        dot_tn(x_ref[1], ahead[0]),
        dot_tn(x_ref[0], go_ref[...]),
    )
    arrive(3)
    dy[2] = (dot_nt(ahead[0], down(2)) + dot_nt(ahead[1], down(0))).astype(BF16)
    dy[3] = dot_nt(ahead[1], down(1)).astype(BF16)
    for k in range(2):
        put(1, k * chans, dot_tn(hid[0], dy[2 - k]) + dot_tn(hid[1], dy[3 - k]))
    pairs = (dot_tn(hid[0], ahead[1]), dot_tn(hid[1], ahead[1])) + near_pairs
    coarse = [pair.astype(BF16) for pair in pairs]
    fine = [(pair - part.astype(F32)).astype(BF16) for pair, part in zip(pairs, coarse)]
    for k in range(3):
        acc = direct[k]
        for n in range(3):
            acc += dot_tn(temporal(n), coarse[k + n]) + dot_tn(temporal(n), fine[k + n])
        put(2, k * chans, acc)
    give_core(1)
    for f in range(2):
        back = jnp.zeros((cells, chans), F32)
        for k in range(3):
            back += dot_nt(dy[f + 2 - k], temporal(k))
        value = pre[f]
        gate = 1.0 / (1.0 + jnp.exp(-value))
        a_pad[f, cols : cells + cols] = (back * gate * (1.0 + value * (1.0 - gate))).astype(BF16)
    start(4)
    start(5)

    give_group(1)
    for i in range(3):
        for j in range(3):
            acc = jnp.zeros((chans, chans), F32)
            for f in range(2):
                acc += dot_tn(
                    x_shift[f, i * cols : i * cols + cells, j * chans : (j + 1) * chans],
                    a_pad[f, cols : cells + cols, :],
                )
            put(0, (3 * i + j) * chans, acc)
    give_core(0)
    give_band(1)
    give_group(0)
    arrive(4)
    arrive(5)
    shift(a_pad, a_shift, (2, 1, 0))
    for f in range(2):
        acc = dy[f].astype(F32)
        for i in range(3):
            for j in range(3):
                tap = 3 * i + j
                acc += dot_nt(
                    a_shift[f, (2 - i) * cols : (2 - i) * cols + cells, j * chans : (j + 1) * chans],
                    ws_ref[tap * chans : (tap + 1) * chans, :],
                )
        latent_ref[f] = acc.astype(BF16)

    give_band(0)
    finish(1)
    finish(0)
    for n in range(6):
        sent(n)
    for p in range(2):
        for copy in core_copies[p] + group_copies[p] + band_copies[p]:
            copy.wait_send()


def per_device(clip_latent, grad_out, w_spatial, w_temporal, w_down):
    clips, frames, height, cols, chans = clip_latent.shape
    groups = lax.axis_size("tm")
    bands = lax.axis_size("space")
    assert clips == 1 and frames == 2 and grad_out.shape[1] == 1 and lax.axis_size("dp") == 2
    count = clips * frames * height * cols * 2 * groups * bands
    scale = 1.0 / math.sqrt(count)
    cells = height * cols
    padded = cells + 2 * cols
    sizes = (9 * chans // (2 * groups), 3 * chans // (2 * groups), 3 * chans // (2 * groups))
    rows = (round_up(sizes[0], 16), round_up(sizes[1] + sizes[2], 16))
    wide = tuple(round_up(size, 128) for size in rows)
    share = chans // bands
    dma = pltpu.SemaphoreType.DMA
    vmem = pl.BlockSpec(memory_space=pltpu.VMEM)
    latent, spatial, temporal, down = pl.pallas_call(
        functools.partial(block_kernel, groups, bands, cols, scale),
        out_shape=(
            jax.ShapeDtypeStruct((2, cells, chans), BF16),
            jax.ShapeDtypeStruct((share, sizes[0]), F32),
            jax.ShapeDtypeStruct((share, sizes[1]), F32),
            jax.ShapeDtypeStruct((share, sizes[2]), F32),
        ),
        in_specs=[pl.BlockSpec(memory_space=pltpu.HBM)] * 5,
        out_specs=(vmem, vmem, vmem, vmem),
        scratch_shapes=[
            pltpu.VMEM((2, cells, chans), BF16),
            pltpu.VMEM((cells, chans), BF16),
            pltpu.VMEM(w_spatial.shape, BF16),
            pltpu.VMEM(w_temporal.shape, BF16),
            pltpu.VMEM(w_down.shape, BF16),
            dma((5,)),
            pltpu.VMEM((2, padded, chans), BF16),
            pltpu.VMEM((2, padded, 3 * chans), BF16),
            pltpu.VMEM((2, padded, chans), BF16),
            pltpu.VMEM((2, padded, 3 * chans), BF16),
            pltpu.VMEM((2, cells, chans), F32),
            pltpu.VMEM((2, cells, chans), BF16),
            pltpu.VMEM((2, cells, chans), BF16),
            pltpu.VMEM((4, cells, chans), BF16),
            pltpu.VMEM((2, groups, rows[0], chans), F32),
            pltpu.VMEM((2, groups, rows[1], chans), F32),
            pltpu.VMEM((groups, rows[0], chans), BF16),
            pltpu.VMEM((groups, rows[1], chans), BF16),
            pltpu.VMEM((groups, rows[0], chans), BF16),
            pltpu.VMEM((groups, rows[1], chans), BF16),
            pltpu.VMEM((groups - 1, rows[0], chans), BF16),
            pltpu.VMEM((groups - 1, rows[1], chans), BF16),
            pltpu.VMEM((groups - 1, rows[0], chans), BF16),
            pltpu.VMEM((groups - 1, rows[1], chans), BF16),
            pltpu.VMEM((wide[0], chans), F32),
            pltpu.VMEM((wide[1], chans), F32),
            pltpu.VMEM((bands, share, wide[0]), BF16),
            pltpu.VMEM((bands, share, wide[1]), BF16),
            pltpu.VMEM((bands, share, wide[0]), F32),
            pltpu.VMEM((bands, share, wide[1]), F32),
            pltpu.VMEM((bands - 1, share, wide[0]), BF16),
            pltpu.VMEM((bands - 1, share, wide[1]), BF16),
            dma((6,)),
            dma((6,)),
            dma((2, groups)),
            dma((2, groups)),
            dma((2, groups - 1)),
            dma((2, groups - 1)),
            dma((2, bands - 1)),
            dma((2, bands - 1)),
        ],
        compiler_params=pltpu.CompilerParams(
            collective_id=0, has_side_effects=True, vmem_limit_bytes=58 * 1024 * 1024
        ),
    )(
        clip_latent.reshape(2, cells, chans),
        grad_out.reshape(cells, chans),
        w_spatial,
        w_temporal,
        w_down,
    )
    return (
        latent.reshape(clip_latent.shape),
        spatial,
        temporal,
        down,
    )


def solution(mesh):
    placed = (P("dp", "tm", "space", None, None), P("dp", "tm", "space", None, None), P(), P(), P())
    return jax.shard_map(
        per_device,
        mesh=mesh,
        in_specs=placed,
        out_specs=(
            P("dp", "tm", "space", None, None),
            P("space", ("dp", "tm")),
            P("space", ("dp", "tm")),
            P("space", ("dp", "tm")),
        ),
        check_vma=False,
    )
```
